256 devices in a mesh: blk: 16 (over x, y_hi, core), rep: 16 (over y_lo, z).
Axes of the slice: x: 4, y: 4 (y_hi: 2, y_lo: 2; y = y_hi * 2 + y_lo), z: 8, core: 2. Of those that a mesh axis runs over, the one named last changes fastest.
Arguments:
- tokens: bfloat16 [32768, 2048], P(('blk', 'rep')), may hold values from -24 to 24
- grad_out: bfloat16 [32768, 2048], P(('blk', 'rep')), may hold values from -1 to 1
- expert_ids: int32 [32768, 2], P(('blk', 'rep')), may hold values from 0 to 15, all different within a row; in each aligned block of 128 rows (0 to 127, 128 to 255, ...) at most 32 rows name the same one
- gates: bfloat16 [32768, 2], P(('blk', 'rep')), may hold values from 0.099609375 to 1
- gate_up_weight: bfloat16 [16, 2048, 1536], P('blk'), may hold values from -0.125 to 0.125
- down_weight: bfloat16 [16, 2048, 768], P('blk'), may hold values from -0.21875 to 0.21875
Outputs:
- grad_tokens: bfloat16 [32768, 2048], P(('blk', 'rep'))
- grad_gates: bfloat16 [32768, 2], P(('blk', 'rep'))
- grad_gate_up: float32 [16, 2048, 1536], P('blk', 'rep')
- grad_down: float32 [16, 2048, 768], P('blk', 'rep')
The draws below stay inside these ranges and needn't reach their ends.
Inputs may be any that keep to these rules, and one draw needn't show every extreme that they name: `expert_ids`: the 2 experts of a token differ. Among the rows of one device, no expert is named more than 32 times.
All inputs are finite; a program needn't handle non-finite values.
Results may differ from the reference program's by a relative error of at most 0.0065.
Values may be sent and summed in bfloat16 or wider, within the bound.
No kernel may reach another device: no remote copies, remote signals or barrier semaphores. Data moves between devices by JAX's collectives and lax.ppermute only.
A program may use at most 192 MiB of HBM per device.

```python
import math
import jax
import jax.numpy as jnp
import numpy as np
from jax import lax

D = 2048
HID = 768
TOP = 2
TOK_DEV = 128
EXPERTS = 16
CAP = 32
TOKENS = 32768
N_BLK = 16
N_REP = 16


def raised(array, key, source, target, shards_of, factor):
    def block_of(dim):
        return (jnp.arange(array.shape[dim]) // (array.shape[dim] // shards_of)).reshape((-1,) + (1,) * (array.ndim - 1 - dim))

    first = jax.random.permutation(key, shards_of)[block_of(target)]
    second = (block_of(target) + shards_of // 2) % shards_of
    return jnp.where((block_of(source) == first) | (block_of(source) == second), factor * array, array)


def steps_of(key, extent, pieces, least, largest):
    def one(axis_at, parts):
        steps = jax.random.uniform(jax.random.fold_in(jax.random.fold_in(key, 6), axis_at), (parts,), jnp.float32, least / len(pieces), largest / len(pieces))
        return jnp.repeat(jnp.exp(steps), extent[axis_at] // parts).reshape((-1,) + (1,) * (len(extent) - axis_at - 1))

    factor_of = one(*pieces[0])
    for cut in pieces[1:]:
        factor_of = factor_of * one(*cut)
    return factor_of


def assign_block(own_key, own, number, rows, number_of, top, most, slope):
    order = jax.random.permutation(own_key, number_of)
    packed, ordinary = portions_of(number_of, rows * top, most, slope, True), portions_of(number_of, rows * top, most, slope, False)
    places = jnp.arange(number_of)

    def named(lengths, offset_by):
        used = int((lengths > 0).sum())
        fixed = max(1, used // 4)
        passed = fixed + (places - fixed + offset_by * (used - fixed)) % max(1, number_of - fixed)
        return jnp.zeros((number_of,), jnp.int32).at[order[jnp.where(places < fixed, places, passed)]].set(jnp.asarray(lengths, jnp.int32))

    lengths = jnp.where(number % 4 == 0, named(packed, number // 4), named(ordinary, number - number // 4 - 1))
    mixed = jax.random.permutation(jax.random.fold_in(own, 3), number_of)
    giver, receiver = mixed[0:number_of // 2 * 2:2], mixed[1:number_of // 2 * 2:2]
    margin = jnp.minimum(lengths[giver] - 1, most - lengths[receiver]) // 2
    margin = jnp.where((giver == order[0]) | (receiver == order[0]) | (lengths[receiver] == 0), 0, jnp.maximum(margin, 0))
    passed = jax.random.randint(jax.random.fold_in(own, 4), (number_of // 2,), 0, 1 << 20) % (margin + 1)
    lengths = lengths.at[giver].add(-passed).at[receiver].add(passed)
    labels = jnp.searchsorted(jnp.cumsum(lengths), jnp.arange(rows * top), side="right").astype(jnp.int32)
    table = labels.reshape(top, rows).T
    table = table[jax.random.permutation(jax.random.fold_in(own, 1), rows)]
    offset_by = jax.random.randint(jax.random.fold_in(own, 2), (rows, 1), 0, top)
    return jnp.take_along_axis(table, (jnp.arange(top)[None, :] + offset_by) % top, axis=1)


def portions_of(amount, total, bound, lean, full):
    loads = [(1 << 20) // math.isqrt(rank ** lean) + 1 for rank in range(1, amount + 1)]
    largest = bound if full else min(bound, max(-(-total // amount), total * loads[0] // sum(loads)))
    least = 1 if total - largest >= amount - 1 else 0
    holding, surplus = [largest] + [least] * (amount - 1), total - largest - least * (amount - 1)
    while surplus > 0:
        movable = [i for i in range(1, amount) if holding[i] < largest] or [i for i in range(1, amount) if holding[i] < bound]
        pool, left = sum([loads[i] for i in movable]), surplus
        for i in movable:
            more = min(bound - holding[i], max(1, left * loads[i] // pool), surplus)
            holding[i] = holding[i] + more
            surplus = surplus - more
    return np.array(holding)


def centred(own_key, shape, width, limit, split=(), kind=jnp.bfloat16):
    array = jax.random.normal(own_key, shape, jnp.float32) * width
    if len(split) > 0:
        array = steps_of(own_key, shape, split, -0.22, 0.18) * array
    return jnp.clip(array, min=-limit, max=limit).astype(kind)


def noise_with(own_key, extent, spread, limit, pieces, heavy, held_as=jnp.bfloat16):
    entries = spread * jax.random.normal(own_key, extent, jnp.float32)
    if pieces:
        entries = entries * steps_of(own_key, extent, pieces, -0.22, 0.18)
    return jnp.clip(raised(entries, jax.random.fold_in(own_key, 3), *heavy), -limit, limit).astype(held_as)


def setup_inputs(seed: int = 0) -> dict:
    keys = jax.random.split(jax.random.key(seed), 7)
    tokens = noise_with(keys[0], (TOKENS, D), 1.0, 24.0, ((0, 256),), (0, 1, 256, 6.0))
    grad_out = centred(keys[1], (TOKENS, D), 0.125, 1.0, ((0, 256),))
    expert_ids_keys = jax.random.split(jax.random.fold_in(keys[2], 1), TOKENS // TOK_DEV)
    expert_ids_turns = jax.random.permutation(jax.random.fold_in(keys[2], 3), TOKENS // TOK_DEV)
    expert_ids = jax.vmap(lambda own, number: assign_block(jax.random.fold_in(keys[2], 2), own, number, TOK_DEV, EXPERTS, TOP, CAP, 2))(expert_ids_keys, expert_ids_turns).reshape((TOKENS, TOP))
    gates = jnp.clip(jnp.exp(math.log(1.0) - 2.306499 * jax.random.uniform(keys[3], (TOKENS, TOP), jnp.float32) ** steps_of(keys[3], (TOKENS, TOP), ((0, 256),), -0.2, 0.2)), 0.099609375, 1.0).astype(jnp.bfloat16)
    gate_up_weight = centred(keys[4], (EXPERTS, D, 2 * HID), D ** -0.5, 0.125, ((0, 16),))
    down_weight = centred(keys[5], (EXPERTS, D, HID), HID ** -0.5, 0.21875, ((0, 16),))
    return {"tokens": tokens, "grad_out": grad_out, "expert_ids": expert_ids, "gates": gates, "gate_up_weight": gate_up_weight, "down_weight": down_weight}


def expert_rows(row_inputs, row_grads, row_gates, gate_matrix, down_matrix):
    projected = jnp.dot(row_inputs, gate_matrix, preferred_element_type=jnp.float32)
    hidden_width = down_matrix.shape[1]
    gate_part = projected[:, :hidden_width]
    up_part = projected[:, hidden_width:]
    sigmoid_gate = jax.nn.sigmoid(gate_part)
    silu_gate = gate_part * sigmoid_gate
    hidden = (silu_gate * up_part).astype(jnp.bfloat16)
    expert_out = lax.dot_general(hidden, down_matrix, (((1,), (1,)), ((), ())), preferred_element_type=jnp.float32)
    gate_grad = jnp.sum(row_grads.astype(jnp.float32) * expert_out, axis=1).astype(jnp.bfloat16)
    scaled = (row_gates.astype(jnp.float32)[:, None] * row_grads.astype(jnp.float32)).astype(jnp.bfloat16)
    grad_hidden = jnp.dot(scaled, down_matrix, preferred_element_type=jnp.float32)
    grad_gate_part = grad_hidden * up_part * sigmoid_gate * (1.0 + gate_part * (1.0 - sigmoid_gate))
    grad_up_part = grad_hidden * silu_gate
    grad_pre = jnp.concatenate([grad_gate_part, grad_up_part], axis=1).astype(jnp.bfloat16)
    row_grad = lax.dot_general(grad_pre, gate_matrix, (((1,), (1,)), ((), ())), preferred_element_type=jnp.float32).astype(jnp.bfloat16)
    return hidden, scaled, grad_pre, row_grad, gate_grad


def reference(tokens, grad_out, expert_ids, gates, gate_up_weight, down_weight):
    flat_ids = expert_ids.reshape(-1).astype(jnp.int32)
    flat_gates = gates.reshape(-1)
    row_bound = N_BLK * N_REP * CAP

    def per_expert(totals, expert):
        input_total, gate_total = totals
        is_chosen = flat_ids == expert
        chosen = jnp.nonzero(is_chosen, size=row_bound, fill_value=0)[0].astype(jnp.int32)
        row_total = jnp.sum(is_chosen.astype(jnp.int32))
        is_valid = jnp.arange(row_bound, dtype=jnp.int32) < row_total
        token_index = (chosen // TOP).astype(jnp.int32)
        row_inputs = tokens[token_index]
        row_grads = jnp.where(is_valid[:, None], grad_out[token_index], jnp.zeros((), grad_out.dtype))
        row_gates = jnp.where(is_valid, flat_gates[chosen], jnp.zeros((), gates.dtype))
        hidden, scaled, grad_pre, row_grad, gate_grad = expert_rows(row_inputs, row_grads, row_gates, gate_up_weight[expert], down_weight[expert])
        input_total = input_total.at[token_index].add(row_grad.astype(jnp.float32))
        gate_total = gate_total.at[chosen].add(jnp.where(is_valid, gate_grad.astype(jnp.float32), jnp.zeros((), jnp.float32)))
        gate_up_grad = lax.dot_general(row_inputs, grad_pre, (((0,), (0,)), ((), ())), preferred_element_type=jnp.float32)
        down_grad = lax.dot_general(scaled, hidden, (((0,), (0,)), ((), ())), preferred_element_type=jnp.float32)
        return (input_total, gate_total), (gate_up_grad, down_grad)

    start_totals = (jnp.zeros((TOKENS, D), jnp.float32), jnp.zeros((TOKENS * TOP,), jnp.float32))
    final_totals, weight_grads = lax.scan(per_expert, start_totals, jnp.arange(EXPERTS, dtype=jnp.int32))
    grad_tokens = final_totals[0].astype(jnp.bfloat16)
    grad_gates = final_totals[1].reshape(TOKENS, TOP).astype(jnp.bfloat16)
    return grad_tokens, grad_gates, weight_grads[0], weight_grads[1]
```

```python
import functools

import jax
import jax.numpy as jnp
from jax import lax
from jax.experimental import pallas as pl
from jax.experimental.pallas import tpu as pltpu
from jax.sharding import PartitionSpec as P

BF16 = jnp.bfloat16
F32 = jnp.float32
LANES = 128
MIB = 1024 * 1024


def dot(left, right, left_dim=1, right_dim=0):
    return lax.dot_general(
        left, right, (((left_dim,), (right_dim,)), ((), ())), preferred_element_type=F32
    )


def dispatch_kernel(ids_ref, gates_ref, tokens_ref, grads_ref, send_ref, target_ref, *, experts):
    count = ids_ref.shape[1]
    slots = send_ref.shape[0]
    width = tokens_ref.shape[1]
    capacity = slots // experts
    first, second = ids_ref[0:1, :], ids_ref[1:2, :]
    expert = lax.broadcasted_iota(jnp.int32, (experts, count), 0)
    first_hot, second_hot = first == expert, second == expert
    earlier = (
        lax.broadcasted_iota(jnp.int32, (count, count), 0)
        < lax.broadcasted_iota(jnp.int32, (count, count), 1)
    ).astype(F32).astype(BF16)
    first_count, second_count = first_hot.astype(F32), second_hot.astype(F32)
    first_before = dot(first_count.astype(BF16), earlier)
    second_before = dot(second_count.astype(BF16), earlier) + jnp.sum(
        first_count, axis=1, keepdims=True
    )
    first_slot = first * capacity + jnp.sum(
        first_count * first_before, axis=0, keepdims=True
    ).astype(jnp.int32)
    second_slot = second * capacity + jnp.sum(
        second_count * second_before, axis=0, keepdims=True
    ).astype(jnp.int32)
    target_ref[0:1, :] = first_slot
    target_ref[1:2, :] = second_slot
    slot = lax.broadcasted_iota(jnp.int32, (slots, count), 0)
    gates = gates_ref[...].astype(F32)
    from_first, from_second = slot == first_slot, slot == second_slot
    pick = jnp.where(from_first | from_second, 1.0, 0.0).astype(BF16)
    scale = jnp.where(
        from_first, gates[0:1, :], jnp.where(from_second, gates[1:2, :], 0.0)
    ).astype(BF16)
    step = 512
    for at in range(0, width, step):
        send_ref[:, at : at + step] = dot(pick, tokens_ref[:, at : at + step]).astype(BF16)
        send_ref[:, width + at : width + at + step] = dot(
            scale, grads_ref[:, at : at + step]
        ).astype(BF16)


def rows_kernel(rows_ref, gate_ref, up_ref, down_ref, hidden_ref, pre_gate_ref, pre_up_ref, gate_sum_ref):
    width = down_ref.shape[0]
    inputs, scaled = rows_ref[:, :width], rows_ref[:, width:]
    gate_part = dot(inputs, gate_ref[...])
    up_part = dot(inputs, up_ref[...])
    grad_hidden = dot(scaled, down_ref[...])
    sigmoid_gate = jax.nn.sigmoid(gate_part)
    silu_gate = gate_part * sigmoid_gate
    hidden = silu_gate * up_part
    hidden_ref[...] = hidden.astype(BF16)
    pre_gate_ref[...] = (
        grad_hidden * up_part * sigmoid_gate * (1.0 + gate_part * (1.0 - sigmoid_gate))
    ).astype(BF16)
    pre_up_ref[...] = (grad_hidden * silu_gate).astype(BF16)
    total = jnp.broadcast_to(
        jnp.sum(hidden * grad_hidden, axis=1, keepdims=True), gate_sum_ref.shape
    )

    @pl.when(pl.program_id(0) == 0)
    def _():
        gate_sum_ref[...] = total

    @pl.when(pl.program_id(0) > 0)
    def _():
        gate_sum_ref[...] += total


def grads_kernel(
    inputs_ref, scaled_ref, hidden_ref, pre_gate_ref, pre_up_ref, gate_ref, up_ref, gate_sum_ref,
    back_ref, weight_ref,
):
    hid = hidden_ref.shape[1]
    step = inputs_ref.shape[1]
    at = pl.multiple_of(pl.program_id(0) * step, step)
    pre_gate, pre_up = pre_gate_ref[...], pre_up_ref[...]
    back_ref[:, pl.ds(at, step)] = (
        dot(pre_gate, gate_ref[...], 1, 1) + dot(pre_up, up_ref[...], 1, 1)
    ).astype(BF16)
    inputs = inputs_ref[...]
    weight_ref[:, :hid] = dot(inputs, pre_gate, 0, 0).astype(BF16)
    weight_ref[:, hid : 2 * hid] = dot(inputs, pre_up, 0, 0).astype(BF16)
    weight_ref[:, 2 * hid :] = dot(scaled_ref[...], hidden_ref[...], 0, 0).astype(BF16)

    @pl.when(pl.program_id(0) == 0)
    def _():
        back_ref[:, back_ref.shape[1] - LANES :] = gate_sum_ref[...].astype(BF16)


def home_kernel(target_ref, gates_ref, back_ref, grads_ref, gate_grads_ref):
    slots, count = back_ref.shape[0], target_ref.shape[1]
    width = grads_ref.shape[1]
    slot = lax.broadcasted_iota(jnp.int32, (slots, count), 0)
    from_first = jnp.where(slot == target_ref[0:1, :], 1.0, 0.0).astype(BF16)
    from_second = jnp.where(slot == target_ref[1:2, :], 1.0, 0.0).astype(BF16)
    both = from_first + from_second
    step = 512
    for at in range(0, width, step):
        grads_ref[:, at : at + step] = dot(both, back_ref[:, at : at + step], 0, 0).astype(BF16)
    sums = back_ref[:, width:]
    first = dot(sums, from_first, 0, 0)[0:1, :]
    second = dot(sums, from_second, 0, 0)[0:1, :]
    gates = gates_ref[...].astype(F32)
    gate_grads_ref[0:1, :] = (first / gates[0:1, :]).astype(BF16)
    gate_grads_ref[1:2, :] = (second / gates[1:2, :]).astype(BF16)


def whole(shape):
    return pl.BlockSpec(shape, lambda i: (0,) * len(shape))


def shards(tokens, grad_out, expert_ids, gates, gate_up_weight, down_weight):
    count, top = expert_ids.shape
    width = tokens.shape[1]
    experts = lax.axis_size("blk")
    capacity = 2 * count * top // experts
    slots = experts * capacity
    gate_up, down = gate_up_weight[0], down_weight[0]
    hid = down.shape[1]
    ids_t, gates_t = expert_ids.T, gates.T
    params = functools.partial(pltpu.CompilerParams, vmem_limit_bytes=48 * MIB)

    send, target = pl.pallas_call(
        functools.partial(dispatch_kernel, experts=experts),
        out_shape=(
            jax.ShapeDtypeStruct((slots, 2 * width), BF16),
            jax.ShapeDtypeStruct((top, count), jnp.int32),
        ),
        compiler_params=params(),
        name="dispatch",
    )(ids_t, gates_t, tokens, grad_out)

    rows = lax.all_to_all(
        send.reshape(experts, capacity, 2 * width), "blk", split_axis=0, concat_axis=0, tiled=True
    ).reshape(slots, 2 * width)

    tile = 256
    steps = hid // tile
    hidden, pre_gate, pre_up, gate_sum = pl.pallas_call(
        rows_kernel,
        grid=(steps,),
        in_specs=[
            whole((slots, 2 * width)),
            pl.BlockSpec((width, tile), lambda i: (0, i)),
            pl.BlockSpec((width, tile), lambda i: (0, steps + i)),
            pl.BlockSpec((width, tile), lambda i: (0, i)),
        ],
        out_specs=[pl.BlockSpec((slots, tile), lambda i: (0, i))] * 3 + [whole((slots, LANES))],
        out_shape=[jax.ShapeDtypeStruct((slots, hid), BF16)] * 3
        + [jax.ShapeDtypeStruct((slots, LANES), F32)],
        compiler_params=params(),
        name="rows",
    )(rows, gate_up, gate_up, down)

    tile = 512
    steps = width // tile
    back, weight = pl.pallas_call(
        grads_kernel,
        grid=(steps,),
        in_specs=[
            pl.BlockSpec((slots, tile), lambda i: (0, i)),
            pl.BlockSpec((slots, tile), lambda i: (0, steps + i)),
            whole((slots, hid)),
            whole((slots, hid)),
            whole((slots, hid)),
            pl.BlockSpec((tile, hid), lambda i: (i, 0)),
            pl.BlockSpec((tile, hid), lambda i: (i, 1)),
            whole((slots, LANES)),
        ],
        out_specs=[whole((slots, width + LANES)), pl.BlockSpec((tile, 3 * hid), lambda i: (i, 0))],
        out_shape=[
            jax.ShapeDtypeStruct((slots, width + LANES), BF16),
            jax.ShapeDtypeStruct((width, 3 * hid), BF16),
        ],
        compiler_params=params(),
        name="grads",
    )(rows, rows, hidden, pre_gate, pre_up, gate_up, gate_up, gate_sum)

    weight_total = lax.psum_scatter(weight, "rep", scatter_dimension=0, tiled=True).astype(F32)
    returned = lax.all_to_all(
        back.reshape(experts, capacity, width + LANES), "blk", split_axis=0, concat_axis=0, tiled=True
    ).reshape(slots, width + LANES)

    grad_tokens, gate_grads = pl.pallas_call(
        home_kernel,
        out_shape=(
            jax.ShapeDtypeStruct((count, width), BF16),
            jax.ShapeDtypeStruct((top, count), BF16),
        ),
        compiler_params=params(),
        name="home",
    )(target, gates_t, returned)
    return (
        grad_tokens,
        gate_grads.T,
        weight_total[None, :, : 2 * hid],
        weight_total[None, :, 2 * hid :],
    )


def solution(mesh):
    in_specs = (
        P(("blk", "rep"), None),
        P(("blk", "rep"), None),
        P(("blk", "rep"), None),
        P(("blk", "rep"), None),
        P("blk", None, None),
        P("blk", None, None),
    )
    out_specs = (
        P(("blk", "rep"), None),
        P(("blk", "rep"), None),
        P("blk", "rep", None),
        P("blk", "rep", None),
    )
    return jax.shard_map(shards, mesh=mesh, in_specs=in_specs, out_specs=out_specs, check_vma=False)
```

```python
import functools

import jax
import jax.numpy as jnp
from jax import lax
from jax.experimental import pallas as pl
from jax.experimental.pallas import tpu as pltpu
from jax.sharding import PartitionSpec as P

BF16 = jnp.bfloat16
F32 = jnp.float32
LANES = 256
MIB = 1024 * 1024
TOTAL_COST = 5_000_000_000


def dot(left, right, left_dim=1, right_dim=0):
    return lax.dot_general(
        left, right, (((left_dim,), (right_dim,)), ((), ())), preferred_element_type=F32
    )


def dispatch_kernel(
    ids_ref, gates_ref, tokens_ref, grads_ref, send_ref, target_ref, place_ref, *, experts, ring
):
    rep = lax.axis_index("rep")
    place_ref[0] = lax.rem(rep, ring)
    place_ref[1] = lax.div(rep, ring)
    count = ids_ref.shape[1]
    slots = send_ref.shape[0]
    width = tokens_ref.shape[1]
    capacity = slots // experts
    first, second = ids_ref[0:1, :], ids_ref[1:2, :]
    expert = lax.broadcasted_iota(jnp.int32, (experts, count), 0)
    first_hot, second_hot = first == expert, second == expert
    earlier = (
        lax.broadcasted_iota(jnp.int32, (count, count), 0)
        < lax.broadcasted_iota(jnp.int32, (count, count), 1)
    ).astype(F32).astype(BF16)
    first_count, second_count = first_hot.astype(F32), second_hot.astype(F32)
    first_before = dot(first_count.astype(BF16), earlier)
    second_before = dot(second_count.astype(BF16), earlier) + jnp.sum(
        first_count, axis=1, keepdims=True
    )
    first_slot = first * capacity + jnp.sum(
        first_count * first_before, axis=0, keepdims=True
    ).astype(jnp.int32)
    second_slot = second * capacity + jnp.sum(
        second_count * second_before, axis=0, keepdims=True
    ).astype(jnp.int32)
    target_ref[0:1, :] = first_slot
    target_ref[1:2, :] = second_slot
    slot = lax.broadcasted_iota(jnp.int32, (slots, count), 0)
    gates = gates_ref[...].astype(F32)
    from_first, from_second = slot == first_slot, slot == second_slot
    pick = jnp.where(from_first | from_second, 1.0, 0.0).astype(BF16)
    scale = jnp.where(
        from_first, gates[0:1, :], jnp.where(from_second, gates[1:2, :], 0.0)
    ).astype(BF16)
    step = 512
    for at in range(0, width, step):
        send_ref[:, at : at + step] = dot(pick, tokens_ref[:, at : at + step]).astype(BF16)
        send_ref[:, width + at : width + at + step] = dot(
            scale, grads_ref[:, at : at + step]
        ).astype(BF16)


def rows_kernel(rows_ref, gate_ref, up_ref, down_ref, hidden_ref, pre_gate_ref, pre_up_ref, gate_sum_ref):
    width = down_ref.shape[0]
    inputs, scaled = rows_ref[:, :width], rows_ref[:, width:]
    gate_part = dot(inputs, gate_ref[...])
    up_part = dot(inputs, up_ref[...])
    grad_hidden = dot(scaled, down_ref[...])
    sigmoid_gate = jax.nn.sigmoid(gate_part)
    silu_gate = gate_part * sigmoid_gate
    hidden = silu_gate * up_part
    hidden_ref[...] = hidden.astype(BF16)
    pre_gate_ref[...] = (
        grad_hidden * up_part * sigmoid_gate * (1.0 + gate_part * (1.0 - sigmoid_gate))
    ).astype(BF16)
    pre_up_ref[...] = (grad_hidden * silu_gate).astype(BF16)
    total = jnp.broadcast_to(
        jnp.sum(hidden * grad_hidden, axis=1, keepdims=True), gate_sum_ref.shape
    )

    @pl.when(pl.program_id(0) == 0)
    def _():
        gate_sum_ref[...] = total

    @pl.when(pl.program_id(0) > 0)
    def _():
        gate_sum_ref[...] += total


def row_grads_kernel(place_ref, pre_gate_ref, pre_up_ref, gate_ref, up_ref, gate_sum_ref, back_ref):
    step = gate_ref.shape[0]
    at = pl.multiple_of(pl.program_id(0) * step, step)
    back_ref[:, pl.ds(at, step)] = (
        dot(pre_gate_ref[...], gate_ref[...], 1, 1) + dot(pre_up_ref[...], up_ref[...], 1, 1)
    ).astype(BF16)

    @pl.when(pl.program_id(0) == 0)
    def _():
        back_ref[:, back_ref.shape[1] - LANES :] = gate_sum_ref[...].astype(BF16)


def add(*terms):
    return sum([term.astype(F32) for term in terms])


def terms_kernel(place_ref, hidden_ref, pre_gate_ref, pre_up_ref, *refs, groups):
    operands = iter(refs[: len(refs) - len(groups)])
    hid = hidden_ref.shape[1]

    def first(inputs, scaled, own):
        return (dot(inputs, pre_gate_ref[...], 0, 0), dot(inputs, pre_up_ref[:, :own], 0, 0))

    def last(inputs, scaled, own):
        return (dot(inputs, pre_up_ref[:, own:], 0, 0), dot(scaled, hidden_ref[...], 0, 0))

    for (items, kind), out_ref in zip(groups, refs[len(refs) - len(groups) :]):
        part = out_ref.shape[-1]
        own = part - hid
        loaded = [
            (next(operands)[...], None if of_first else next(operands)[...])
            + tuple(next(operands) for _ in range(added))
            for _, _, of_first, added in items
        ]
        paired = len(items) == 2 and items[0][2] == items[1][2]
        if paired:
            inputs = jnp.concatenate([loaded[0][0], loaded[1][0]], axis=1)
            scaled = None if items[0][2] else jnp.concatenate([loaded[0][1], loaded[1][1]], axis=1)
            sums = (first if items[0][2] else last)(inputs, scaled, own)
            rows = inputs.shape[1] // 2
            results = [tuple(half[:rows] for half in sums), tuple(half[rows:] for half in sums)]
        else:
            results = [
                (first if item[2] else last)(load[0], load[1], own)
                for item, load in zip(items, loaded)
            ]
        for at, (item, load, result) in enumerate(zip(items, loaded, results)):
            start = 0
            for piece in result:
                end = start + piece.shape[1]
                for added in load[2:]:
                    piece = piece + added[0, :, start:end].astype(F32)
                out_ref[at, :, start:end] = piece.astype(kind)
                start = end


def joined_kernel(place_ref, kept_ref, other_ref, up_out, down_out):
    up_out[0] = add(kept_ref[0], other_ref[0]).astype(BF16)
    down_out[0] = add(kept_ref[1], other_ref[1]).astype(BF16)


def total_kernel(
    place_ref, base_ref, x_up_ref, x_down_ref, y_up_ref, y_down_ref, gate_up_ref, down_ref
):
    part = x_up_ref.shape[-1]
    wide = gate_up_ref.shape[-1]
    last = add(base_ref[1], x_down_ref[0], y_up_ref[0])
    gate_up_ref[0, :, :part] = add(base_ref[0], x_up_ref[0], y_down_ref[0])
    gate_up_ref[0, :, part:] = last[:, : wide - part]
    down_ref[0] = last[:, wide - part :]


def home_kernel(target_ref, gates_ref, back_ref, after_ref, grads_ref, gate_grads_ref):
    slots, count = back_ref.shape[0], target_ref.shape[1]
    width = grads_ref.shape[1]
    slot = lax.broadcasted_iota(jnp.int32, (slots, count), 0)
    from_first = jnp.where(slot == target_ref[0:1, :], 1.0, 0.0).astype(BF16)
    from_second = jnp.where(slot == target_ref[1:2, :], 1.0, 0.0).astype(BF16)
    both = from_first + from_second
    step = 512
    for at in range(0, width, step):
        grads_ref[:, at : at + step] = dot(both, back_ref[:, at : at + step], 0, 0).astype(BF16)
    sums = back_ref[:, width : width + 128]
    first = dot(sums, from_first, 0, 0)[0:1, :]
    second = dot(sums, from_second, 0, 0)[0:1, :]
    gates = gates_ref[...].astype(F32)
    gate_grads_ref[0:1, :] = (first / gates[0:1, :]).astype(BF16)
    gate_grads_ref[1:2, :] = (second / gates[1:2, :]).astype(BF16)


def whole(shape):
    return pl.BlockSpec(shape, lambda i: (0,) * len(shape))


def shards(tokens, grad_out, expert_ids, gates, gate_up_weight, down_weight):
    count, top = expert_ids.shape
    width = tokens.shape[1]
    experts = lax.axis_size("blk")
    capacity = 2 * count * top // experts
    slots = experts * capacity
    gate_up, down = gate_up_weight[0], down_weight[0]
    hid = down.shape[1]
    ids_t, gates_t = expert_ids.T, gates.T
    ring = lax.axis_size("rep") // 2
    params = functools.partial(pltpu.CompilerParams, vmem_limit_bytes=48 * MIB)

    send, target, place = pl.pallas_call(
        functools.partial(dispatch_kernel, experts=experts, ring=ring),
        out_shape=(
            jax.ShapeDtypeStruct((slots, 2 * width), BF16),
            jax.ShapeDtypeStruct((top, count), jnp.int32),
            jax.ShapeDtypeStruct((2,), jnp.int32),
        ),
        out_specs=(
            pl.BlockSpec(memory_space=pltpu.VMEM),
            pl.BlockSpec(memory_space=pltpu.VMEM),
            pl.BlockSpec(memory_space=pltpu.SMEM),
        ),
        compiler_params=params(vmem_limit_bytes=60 * MIB),
        name="dispatch",
    )(ids_t, gates_t, tokens, grad_out)

    rows = lax.all_to_all(
        send.reshape(experts, capacity, 2 * width), "blk", split_axis=0, concat_axis=0, tiled=True
    ).reshape(slots, 2 * width)

    tile = 256
    steps = hid // tile
    hidden, pre_gate, pre_up, gate_sum = pl.pallas_call(
        rows_kernel,
        grid=(steps,),
        in_specs=[
            whole((slots, 2 * width)),
            pl.BlockSpec((width, tile), lambda i: (0, i)),
            pl.BlockSpec((width, tile), lambda i: (0, steps + i)),
            pl.BlockSpec((width, tile), lambda i: (0, i)),
        ],
        out_specs=[pl.BlockSpec((slots, tile), lambda i: (0, i))] * 3 + [whole((slots, LANES))],
        out_shape=[jax.ShapeDtypeStruct((slots, hid), BF16)] * 3
        + [jax.ShapeDtypeStruct((slots, LANES), F32)],
        compiler_params=params(),
        name="rows",
    )(rows, gate_up, gate_up, down)

    block = width // lax.axis_size("rep")

    def around(place, ahead):
        return lax.rem(place[0] + ahead, ring)

    def whole_p(shape):
        return pl.BlockSpec(shape, lambda i, p: (0,) * len(shape))

    anywhere = pl.BlockSpec(memory_space=pl.ANY)

    def call(kernel, name, grid, in_specs, out_specs, out_shape, *operands, after=(), cost=1):
        first = 1 + len(in_specs)

        def body(*refs):
            kernel(*refs[:first], *refs[first + len(after) : -1])
            refs[-1][...] = jnp.zeros_like(refs[-1])

        *outs, token = pl.pallas_call(
            body,
            grid_spec=pltpu.PrefetchScalarGridSpec(
                num_scalar_prefetch=1,
                grid=(grid,),
                in_specs=[*in_specs, *[anywhere] * len(after)],
                out_specs=[*out_specs, whole_p((8, 128))],
            ),
            out_shape=[*out_shape, jax.ShapeDtypeStruct((8, 128), F32)],
            compiler_params=params(),
            cost_estimate=pl.CostEstimate(flops=cost, bytes_accessed=1, transcendentals=0),
            name=name,
        )(place, *operands, *after)
        return outs, token

    def shape(*dims):
        return pltpu.HBM(dims, BF16)

    def permute(array, ahead):
        pairs = [
            (high * ring + low, high * ring + (low + ahead) % ring)
            for high in range(2)
            for low in range(ring)
        ]
        return lax.ppermute(array, "rep", pairs)

    def swap(array):
        pairs = [(at, (at + ring) % (2 * ring)) for at in range(2 * ring)]
        return lax.ppermute(array, "rep", pairs)

    far = ring // 2
    part = 3 * hid // 2

    def onward(pair):
        return permute(pair[0], 1), permute(pair[1], -1)

    def some_terms(name, groups, after=()):
        specs, operands, counted, outs, kinds = [], [], [], [], []
        for items, kind in groups:
            for half, ahead, of_first, added in items:
                for start in (0,) if of_first else (0, 2):

                    def at(i, p, half=half, ahead=ahead, start=start):
                        return 0, (start + half(p)) * ring + around(p, (ahead + ring) % ring)

                    specs.append(pl.BlockSpec((slots, block), at))
                    operands.append(rows)
                for array, place_of in added:

                    def at(i, p, place_of=place_of):
                        return place_of(p), 0, 0

                    specs.append(pl.BlockSpec((1, block, part), at))
                    operands.append(array)
            counted.append(([item[:3] + (len(item[3]),) for item in items], kind))
            outs.append(whole_p((len(items), block, part)))
            kinds.append(
                shape(len(items), block, part)
                if kind == BF16
                else jax.ShapeDtypeStruct((len(items), block, part), kind)
            )
        return call(
            functools.partial(terms_kernel, groups=counted),
            name,
            1,
            [whole_p((slots, hid))] * 3 + specs,
            outs,
            kinds,
            hidden, pre_gate, pre_up, *operands, after=after,
        )

    def low(p):
        return 0

    def high(p):
        return 1

    def mine(p):
        return p[1]

    def theirs(p):
        return 1 - p[1]

    def hop(name, at, up_first, pair, after):
        def both(ahead, of_first, array):
            return [
                (half, ahead, of_first, [] if array is None else [(array, half)])
                for half in (low, high)
            ], BF16

        up, down = pair or (None, None)
        return some_terms(
            name, [both(at, up_first, up), both(-at, not up_first, down)], after
        )

    def split_hop(name, at, up_first, pair, after):
        def one_half(half, kind):
            return [
                (half, at, up_first, [(pair[0], half)]),
                (half, -at, not up_first, [(pair[1], half)]),
            ], kind

        return some_terms(name, [one_half(mine, F32), one_half(theirs, BF16)], after)

    one = whole_p((1, block, part))
    pair_of = whole_p((2, block, part))

    def joined(name, kept, other, after):
        return call(
            joined_kernel,
            name,
            1,
            [pair_of, pair_of],
            [one] * 2,
            [shape(1, block, part)] * 2,
            kept, other, after=after,
        )

    tile = 4 * block
    steps = width // tile
    (sent,), token = some_terms(
        "own_theirs", [([(theirs, 0, True, []), (theirs, 0, False, [])], BF16)]
    )
    own_other = swap(sent)
    sent, token = hop("first_x", far, True, None, (token,))
    x_pair = onward(sent)
    sent, token = hop("first_y", far - 1, False, None, (token,))
    y_pair = onward(sent)
    (base,), token = some_terms(
        "own",
        [
            (
                [
                    (mine, 0, True, [(own_other, low)]),
                    (mine, 0, False, [(own_other, high)]),
                ],
                F32,
            )
        ],
        (token,),
    )
    (back,), token = call(
        row_grads_kernel,
        "row_grads",
        steps,
        [
            whole_p((slots, hid)),
            whole_p((slots, hid)),
            pl.BlockSpec((tile, hid), lambda i, p: (i, 0)),
            pl.BlockSpec((tile, hid), lambda i, p: (i, 1)),
            whole_p((slots, LANES)),
        ],
        [whole_p((slots, width + LANES))],
        [shape(slots, width + LANES)],
        pre_gate, pre_up, gate_up, gate_up, gate_sum, after=(token,),
    )
    sent, token = hop("hop_x3", far - 1, True, x_pair, (token,))
    x_pair = onward(sent)
    sent, token = hop("hop_y2", far - 2, False, y_pair, (token,))
    y_pair = onward(sent)
    sent, token = hop("hop_x2", far - 2, True, x_pair, (token,))
    x_pair = onward(sent)
    (y_kept, sent), token = split_hop("hop_y1", far - 3, False, y_pair, (token,))
    y_other = swap(sent)
    (x_kept, sent), token = split_hop("hop_x1", far - 3, True, x_pair, (token,))
    x_other = swap(sent)
    sent, token = joined("joined_y", y_kept, y_other, (token,))
    y_pair = onward(sent)
    sent, token = joined("joined_x", x_kept, x_other, (token,))
    x_pair = onward(sent)
    (gate_up_total, down_total), token = call(
        total_kernel,
        "total",
        1,
        [pair_of, one, one, one, one],
        [whole_p((1, block, 2 * hid)), whole_p((1, block, hid))],
        [
            jax.ShapeDtypeStruct((1, block, 2 * hid), F32),
            jax.ShapeDtypeStruct((1, block, hid), F32),
        ],
        base, *x_pair, *y_pair, cost=TOTAL_COST,
    )

    returned = lax.all_to_all(
        back.reshape(experts, capacity, width + LANES), "blk", split_axis=0, concat_axis=0, tiled=True
    ).reshape(slots, width + LANES)

    grad_tokens, gate_grads = pl.pallas_call(
        home_kernel,
        out_shape=(
            jax.ShapeDtypeStruct((count, width), BF16),
            jax.ShapeDtypeStruct((top, count), BF16),
        ),
        compiler_params=params(),
        name="home",
    )(target, gates_t, returned, token)
    return grad_tokens, gate_grads.T, gate_up_total, down_total


def solution(mesh):
    in_specs = (
        P(("blk", "rep"), None),
        P(("blk", "rep"), None),
        P(("blk", "rep"), None),
        P(("blk", "rep"), None),
        P("blk", None, None),
        P("blk", None, None),
    )
    out_specs = (
        P(("blk", "rep"), None),
        P(("blk", "rep"), None),
        P("blk", "rep", None),
        P("blk", "rep", None),
    )
    return jax.shard_map(shards, mesh=mesh, in_specs=in_specs, out_specs=out_specs, check_vma=False)
```

```python
import functools

import jax
import jax.numpy as jnp
from jax import lax
from jax.experimental import pallas as pl
from jax.experimental.pallas import tpu as pltpu
from jax.sharding import PartitionSpec as P

BF16 = jnp.bfloat16
F32 = jnp.float32
LANES = 128
MIB = 1024 * 1024
TOTAL_COST = 5_000_000_000


def dot(left, right, left_dim=1, right_dim=0):
    return lax.dot_general(
        left, right, (((left_dim,), (right_dim,)), ((), ())), preferred_element_type=F32
    )


def dispatch_kernel(
    ids_ref, gates_ref, tokens_ref, grads_ref, send_ref, target_ref, place_ref, *, experts, ring
):
    rep = lax.axis_index("rep")
    place_ref[0] = lax.rem(rep, ring)
    place_ref[1] = lax.div(rep, ring)
    count = ids_ref.shape[1]
    slots = send_ref.shape[0]
    width = tokens_ref.shape[1]
    capacity = slots // experts
    first, second = ids_ref[0:1, :], ids_ref[1:2, :]
    expert = lax.broadcasted_iota(jnp.int32, (experts, count), 0)
    first_hot, second_hot = first == expert, second == expert
    earlier = (
        lax.broadcasted_iota(jnp.int32, (count, count), 0)
        < lax.broadcasted_iota(jnp.int32, (count, count), 1)
    ).astype(F32).astype(BF16)
    first_count, second_count = first_hot.astype(F32), second_hot.astype(F32)
    first_before = dot(first_count.astype(BF16), earlier)
    second_before = dot(second_count.astype(BF16), earlier) + jnp.sum(
        first_count, axis=1, keepdims=True
    )
    first_slot = first * capacity + jnp.sum(
        first_count * first_before, axis=0, keepdims=True
    ).astype(jnp.int32)
    second_slot = second * capacity + jnp.sum(
        second_count * second_before, axis=0, keepdims=True
    ).astype(jnp.int32)
    target_ref[0:1, :] = first_slot
    target_ref[1:2, :] = second_slot
    slot = lax.broadcasted_iota(jnp.int32, (slots, count), 0)
    gates = gates_ref[...].astype(F32)
    from_first, from_second = slot == first_slot, slot == second_slot
    pick = jnp.where(from_first | from_second, 1.0, 0.0).astype(BF16)
    scale = jnp.where(
        from_first, gates[0:1, :], jnp.where(from_second, gates[1:2, :], 0.0)
    ).astype(BF16)
    step = 512
    for at in range(0, width, step):
        send_ref[:, at : at + step] = dot(pick, tokens_ref[:, at : at + step]).astype(BF16)
        send_ref[:, width + at : width + at + step] = dot(
            scale, grads_ref[:, at : at + step]
        ).astype(BF16)


def rows_kernel(rows_ref, gate_ref, up_ref, down_ref, hidden_ref, pre_gate_ref, pre_up_ref, gate_sum_ref):
    width = down_ref.shape[0]
    inputs, scaled = rows_ref[:, :width], rows_ref[:, width:]
    gate_part = dot(inputs, gate_ref[...])
    up_part = dot(inputs, up_ref[...])
    grad_hidden = dot(scaled, down_ref[...])
    sigmoid_gate = jax.nn.sigmoid(gate_part)
    silu_gate = gate_part * sigmoid_gate
    hidden = silu_gate * up_part
    hidden_ref[...] = hidden.astype(BF16)
    pre_gate_ref[...] = (
        grad_hidden * up_part * sigmoid_gate * (1.0 + gate_part * (1.0 - sigmoid_gate))
    ).astype(BF16)
    pre_up_ref[...] = (grad_hidden * silu_gate).astype(BF16)
    total = jnp.broadcast_to(
        jnp.sum(hidden * grad_hidden, axis=1, keepdims=True), gate_sum_ref.shape
    )

    @pl.when(pl.program_id(0) == 0)
    def _():
        gate_sum_ref[...] = total

    @pl.when(pl.program_id(0) > 0)
    def _():
        gate_sum_ref[...] += total


def row_grads_kernel(place_ref, pre_gate_ref, pre_up_ref, gate_ref, up_ref, gate_sum_ref, back_ref):
    step = gate_ref.shape[0]
    at = pl.multiple_of(pl.program_id(0) * step, step)
    back_ref[:, pl.ds(at, step)] = (
        dot(pre_gate_ref[...], gate_ref[...], 1, 1) + dot(pre_up_ref[...], up_ref[...], 1, 1)
    ).astype(BF16)

    @pl.when(pl.program_id(0) == 0)
    def _():
        back_ref[:, back_ref.shape[1] - LANES :] = gate_sum_ref[...].astype(BF16)


def add(*terms):
    return sum([term.astype(F32) for term in terms])


def terms_kernel(place_ref, hidden_ref, pre_gate_ref, pre_up_ref, *refs, groups):
    operands = iter(refs[: len(refs) - len(groups)])
    hid = hidden_ref.shape[1]

    def first(inputs, scaled, own):
        return (dot(inputs, pre_gate_ref[...], 0, 0), dot(inputs, pre_up_ref[:, :own], 0, 0))

    def last(inputs, scaled, own):
        return (dot(inputs, pre_up_ref[:, own:], 0, 0), dot(scaled, hidden_ref[...], 0, 0))

    for (items, kind), out_ref in zip(groups, refs[len(refs) - len(groups) :]):
        part = out_ref.shape[-1]
        own = part - hid
        loaded = [
            (next(operands)[...], None if of_first else next(operands)[...])
            + tuple(next(operands) for _ in range(added))
            for _, _, of_first, added in items
        ]
        paired = len(items) == 2 and items[0][2] == items[1][2]
        if paired:
            inputs = jnp.concatenate([loaded[0][0], loaded[1][0]], axis=1)
            scaled = None if items[0][2] else jnp.concatenate([loaded[0][1], loaded[1][1]], axis=1)
            sums = (first if items[0][2] else last)(inputs, scaled, own)
            rows = inputs.shape[1] // 2
            results = [tuple(half[:rows] for half in sums), tuple(half[rows:] for half in sums)]
        else:
            results = [
                (first if item[2] else last)(load[0], load[1], own)
                for item, load in zip(items, loaded)
            ]
        for at, (item, load, result) in enumerate(zip(items, loaded, results)):
            start = 0
            for piece in result:
                end = start + piece.shape[1]
                for added in load[2:]:
                    piece = piece + added[0, :, start:end].astype(F32)
                out_ref[at, :, start:end] = piece.astype(kind)
                start = end


def joined_kernel(place_ref, kept_ref, other_ref, up_out, down_out):
    up_out[0] = add(kept_ref[0], other_ref[0]).astype(BF16)
    down_out[0] = add(kept_ref[1], other_ref[1]).astype(BF16)


def total_kernel(
    place_ref, base_ref, x_up_ref, x_down_ref, y_up_ref, y_down_ref, gate_up_ref, down_ref
):
    part = x_up_ref.shape[-1]
    wide = gate_up_ref.shape[-1]
    last = add(base_ref[1], x_down_ref[0], y_up_ref[0])
    gate_up_ref[0, :, :part] = add(base_ref[0], x_up_ref[0], y_down_ref[0])
    gate_up_ref[0, :, part:] = last[:, : wide - part]
    down_ref[0] = last[:, wide - part :]


def home_kernel(target_ref, gates_ref, back_ref, grads_ref, gate_grads_ref):
    slots, count = back_ref.shape[0], target_ref.shape[1]
    width = grads_ref.shape[1]
    slot = lax.broadcasted_iota(jnp.int32, (slots, count), 0)
    from_first = jnp.where(slot == target_ref[0:1, :], 1.0, 0.0).astype(BF16)
    from_second = jnp.where(slot == target_ref[1:2, :], 1.0, 0.0).astype(BF16)
    both = from_first + from_second
    step = 512
    for at in range(0, width, step):
        grads_ref[:, at : at + step] = dot(both, back_ref[:, at : at + step], 0, 0).astype(BF16)
    sums = back_ref[:, width : width + 128]
    first = dot(sums, from_first, 0, 0)[0:1, :]
    second = dot(sums, from_second, 0, 0)[0:1, :]
    gates = gates_ref[...].astype(F32)
    gate_grads_ref[0:1, :] = (first / gates[0:1, :]).astype(BF16)
    gate_grads_ref[1:2, :] = (second / gates[1:2, :]).astype(BF16)


def whole(shape):
    return pl.BlockSpec(shape, lambda i: (0,) * len(shape))


def shards(tokens, grad_out, expert_ids, gates, gate_up_weight, down_weight):
    count, top = expert_ids.shape
    width = tokens.shape[1]
    experts = lax.axis_size("blk")
    capacity = 2 * count * top // experts
    slots = experts * capacity
    gate_up, down = gate_up_weight[0], down_weight[0]
    hid = down.shape[1]
    ids_t, gates_t = expert_ids.T, gates.T
    ring = lax.axis_size("rep") // 2
    params = functools.partial(pltpu.CompilerParams, vmem_limit_bytes=48 * MIB)

    send, target, place = pl.pallas_call(
        functools.partial(dispatch_kernel, experts=experts, ring=ring),
        out_shape=(
            jax.ShapeDtypeStruct((slots, 2 * width), BF16),
            jax.ShapeDtypeStruct((top, count), jnp.int32),
            jax.ShapeDtypeStruct((2,), jnp.int32),
        ),
        out_specs=(
            pl.BlockSpec(memory_space=pltpu.VMEM),
            pl.BlockSpec(memory_space=pltpu.VMEM),
            pl.BlockSpec(memory_space=pltpu.SMEM),
        ),
        compiler_params=params(vmem_limit_bytes=60 * MIB),
        name="dispatch",
    )(ids_t, gates_t, tokens, grad_out)

    rows = lax.all_to_all(
        send.reshape(experts, capacity, 2 * width), "blk", split_axis=0, concat_axis=0, tiled=True
    ).reshape(slots, 2 * width)

    tile = 256
    steps = hid // tile
    hidden, pre_gate, pre_up, gate_sum = pl.pallas_call(
        rows_kernel,
        grid=(steps,),
        in_specs=[
            whole((slots, 2 * width)),
            pl.BlockSpec((width, tile), lambda i: (0, i)),
            pl.BlockSpec((width, tile), lambda i: (0, steps + i)),
            pl.BlockSpec((width, tile), lambda i: (0, i)),
        ],
        out_specs=[pl.BlockSpec((slots, tile), lambda i: (0, i))] * 3 + [whole((slots, LANES))],
        out_shape=[jax.ShapeDtypeStruct((slots, hid), BF16)] * 3
        + [jax.ShapeDtypeStruct((slots, LANES), F32)],
        compiler_params=params(),
        name="rows",
    )(rows, gate_up, gate_up, down)

    block = width // lax.axis_size("rep")

    def around(place, ahead):
        return lax.rem(place[0] + ahead, ring)

    def whole_p(shape):
        return pl.BlockSpec(shape, lambda i, p: (0,) * len(shape))

    anywhere = pl.BlockSpec(memory_space=pl.ANY)

    def call(kernel, name, grid, in_specs, out_specs, out_shape, *operands, after=(), cost=1):
        first = 1 + len(in_specs)

        def body(*refs):
            kernel(*refs[:first], *refs[first + len(after) : -1])
            refs[-1][...] = jnp.zeros_like(refs[-1])

        *outs, token = pl.pallas_call(
            body,
            grid_spec=pltpu.PrefetchScalarGridSpec(
                num_scalar_prefetch=1,
                grid=(grid,),
                in_specs=[*in_specs, *[anywhere] * len(after)],
                out_specs=[*out_specs, whole_p((8, 128))],
            ),
            out_shape=[*out_shape, jax.ShapeDtypeStruct((8, 128), F32)],
            compiler_params=params(),
            cost_estimate=pl.CostEstimate(flops=cost, bytes_accessed=1, transcendentals=0),
            name=name,
        )(place, *operands, *after)
        return outs, token

    def shape(*dims):
        return pltpu.HBM(dims, BF16)

    def permute(array, ahead):
        pairs = [
            (high * ring + low, high * ring + (low + ahead) % ring)
            for high in range(2)
            for low in range(ring)
        ]
        return lax.ppermute(array, "rep", pairs)

    def swap(array):
        pairs = [(at, (at + ring) % (2 * ring)) for at in range(2 * ring)]
        return lax.ppermute(array, "rep", pairs)

    far = ring // 2
    part = 3 * hid // 2

    def onward(pair):
        return permute(pair[0], 1), permute(pair[1], -1)

    def some_terms(name, groups, after=()):
        specs, operands, counted, outs, kinds = [], [], [], [], []
        for items, kind in groups:
            for half, ahead, of_first, added in items:
                for start in (0,) if of_first else (0, 2):

                    def at(i, p, half=half, ahead=ahead, start=start):
                        return 0, (start + half(p)) * ring + around(p, (ahead + ring) % ring)

                    specs.append(pl.BlockSpec((slots, block), at))
                    operands.append(rows)
                for array, place_of in added:

                    def at(i, p, place_of=place_of):
                        return place_of(p), 0, 0

                    specs.append(pl.BlockSpec((1, block, part), at))
                    operands.append(array)
            counted.append(([item[:3] + (len(item[3]),) for item in items], kind))
            outs.append(whole_p((len(items), block, part)))
            kinds.append(
                shape(len(items), block, part)
                if kind == BF16
                else jax.ShapeDtypeStruct((len(items), block, part), kind)
            )
        return call(
            functools.partial(terms_kernel, groups=counted),
            name,
            1,
            [whole_p((slots, hid))] * 3 + specs,
            outs,
            kinds,
            hidden, pre_gate, pre_up, *operands, after=after,
        )

    def low(p):
        return 0

    def high(p):
        return 1

    def mine(p):
        return p[1]

    def theirs(p):
        return 1 - p[1]

    def hop(name, at, up_first, pair, after):
        def both(ahead, of_first, array):
            return [
                (half, ahead, of_first, [] if array is None else [(array, half)])
                for half in (low, high)
            ], BF16

        up, down = pair or (None, None)
        return some_terms(
            name, [both(at, up_first, up), both(-at, not up_first, down)], after
        )

    def split_hop(name, at, up_first, pair, after):
        def one_half(half, kind):
            return [
                (half, at, up_first, [(pair[0], half)]),
                (half, -at, not up_first, [(pair[1], half)]),
            ], kind

        return some_terms(name, [one_half(mine, F32), one_half(theirs, BF16)], after)

    one = whole_p((1, block, part))
    pair_of = whole_p((2, block, part))

    def joined(name, kept, other, after, cost=1):
        return call(
            joined_kernel,
            name,
            1,
            [pair_of, pair_of],
            [one] * 2,
            [shape(1, block, part)] * 2,
            kept, other, after=after, cost=cost,
        )

    tile = 4 * block
    steps = width // tile
    sent, token = hop("first_x", far, True, None, ())
    x_pair = onward(sent)
    (sent,), token = some_terms(
        "own_theirs", [([(theirs, 0, True, []), (theirs, 0, False, [])], BF16)],
        (token,),
    )
    own_other = swap(sent)
    sent, token = hop("first_y", far - 1, False, None, (token,))
    y_pair = onward(sent)
    (back,), token = call(
        row_grads_kernel,
        "row_grads",
        steps,
        [
            whole_p((slots, hid)),
            whole_p((slots, hid)),
            pl.BlockSpec((tile, hid), lambda i, p: (i, 0)),
            pl.BlockSpec((tile, hid), lambda i, p: (i, 1)),
            whole_p((slots, LANES)),
        ],
        [whole_p((slots, width + LANES))],
        [shape(slots, width + LANES)],
        pre_gate, pre_up, gate_up, gate_up, gate_sum, after=(token,),
    )
    sent, token = hop("hop_x3", far - 1, True, x_pair, (token,))
    x_pair = onward(sent)
    sent, token = hop("hop_y2", far - 2, False, y_pair, (token,))
    y_pair = onward(sent)
    (base,), token = some_terms(
        "own",
        [
            (
                [
                    (mine, 0, True, [(own_other, low)]),
                    (mine, 0, False, [(own_other, high)]),
                ],
                F32,
            )
        ],
        (token,),
    )
    sent, token = hop("hop_x2", far - 2, True, x_pair, (token,))
    x_pair = onward(sent)
    (y_kept, sent), token = split_hop("hop_y1", far - 3, False, y_pair, (token,))
    y_other = swap(sent)
    (x_kept, sent), token = split_hop("hop_x1", far - 3, True, x_pair, (token,))
    x_other = swap(sent)
    sent, token = joined("joined_y", y_kept, y_other, (token,))
    y_pair = onward(sent)
    sent, token = joined("joined_x", x_kept, x_other, (token,), TOTAL_COST)
    x_pair = onward(sent)
    (gate_up_total, down_total), _ = call(
        total_kernel,
        "total",
        1,
        [pair_of, one, one, one, one],
        [whole_p((1, block, 2 * hid)), whole_p((1, block, hid))],
        [
            jax.ShapeDtypeStruct((1, block, 2 * hid), F32),
            jax.ShapeDtypeStruct((1, block, hid), F32),
        ],
        base, *x_pair, *y_pair,
    )

    returned = lax.all_to_all(
        back.reshape(experts, capacity, width + LANES), "blk", split_axis=0, concat_axis=0, tiled=True
    ).reshape(slots, width + LANES)

    grad_tokens, gate_grads = pl.pallas_call(
        home_kernel,
        out_shape=(
            jax.ShapeDtypeStruct((count, width), BF16),
            jax.ShapeDtypeStruct((top, count), BF16),
        ),
        compiler_params=params(),
        name="home",
    )(target, gates_t, returned)
    return grad_tokens, gate_grads.T, gate_up_total, down_total


def solution(mesh):
    in_specs = (
        P(("blk", "rep"), None),
        P(("blk", "rep"), None),
        P(("blk", "rep"), None),
        P(("blk", "rep"), None),
        P("blk", None, None),
        P("blk", None, None),
    )
    out_specs = (
        P(("blk", "rep"), None),
        P(("blk", "rep"), None),
        P("blk", "rep", None),
        P("blk", "rep", None),
    )
    return jax.shard_map(shards, mesh=mesh, in_specs=in_specs, out_specs=out_specs, check_vma=False)
```

```python
import functools

import jax
import jax.numpy as jnp
from jax import lax
from jax.experimental import pallas as pl
from jax.experimental.pallas import tpu as pltpu
from jax.sharding import PartitionSpec as P

BF16 = jnp.bfloat16
F32 = jnp.float32
LANES = 128
MIB = 1024 * 1024
TOTAL_COST = 5_000_000_000


def dot(left, right, left_dim=1, right_dim=0):
    return lax.dot_general(
        left, right, (((left_dim,), (right_dim,)), ((), ())), preferred_element_type=F32
    )


def dispatch_kernel(
    ids_ref, gates_ref, tokens_ref, grads_ref, send_ref, target_ref, place_ref, *, experts, ring
):
    rep = lax.axis_index("rep")
    place_ref[0] = lax.rem(rep, ring)
    place_ref[1] = lax.div(rep, ring)
    count = ids_ref.shape[1]
    slots = send_ref.shape[0]
    width = tokens_ref.shape[1]
    capacity = slots // experts
    first, second = ids_ref[0:1, :], ids_ref[1:2, :]
    expert = lax.broadcasted_iota(jnp.int32, (experts, count), 0)
    first_hot, second_hot = first == expert, second == expert
    earlier = (
        lax.broadcasted_iota(jnp.int32, (count, count), 0)
        < lax.broadcasted_iota(jnp.int32, (count, count), 1)
    ).astype(F32).astype(BF16)
    first_count, second_count = first_hot.astype(F32), second_hot.astype(F32)
    first_before = dot(first_count.astype(BF16), earlier)
    second_before = dot(second_count.astype(BF16), earlier) + jnp.sum(
        first_count, axis=1, keepdims=True
    )
    first_slot = first * capacity + jnp.sum(
        first_count * first_before, axis=0, keepdims=True
    ).astype(jnp.int32)
    second_slot = second * capacity + jnp.sum(
        second_count * second_before, axis=0, keepdims=True
    ).astype(jnp.int32)
    target_ref[0:1, :] = first_slot
    target_ref[1:2, :] = second_slot
    slot = lax.broadcasted_iota(jnp.int32, (slots, count), 0)
    gates = gates_ref[...].astype(F32)
    from_first, from_second = slot == first_slot, slot == second_slot
    pick = jnp.where(from_first | from_second, 1.0, 0.0).astype(BF16)
    scale = jnp.where(
        from_first, gates[0:1, :], jnp.where(from_second, gates[1:2, :], 0.0)
    ).astype(BF16)
    step = 512
    for at in range(0, width, step):
        send_ref[:, at : at + step] = dot(pick, tokens_ref[:, at : at + step]).astype(BF16)
        send_ref[:, width + at : width + at + step] = dot(
            scale, grads_ref[:, at : at + step]
        ).astype(BF16)


def rows_kernel(rows_ref, gate_ref, up_ref, down_ref, hidden_ref, pre_gate_ref, pre_up_ref, gate_sum_ref):
    width = down_ref.shape[0]
    inputs, scaled = rows_ref[:, :width], rows_ref[:, width:]
    gate_part = dot(inputs, gate_ref[...])
    up_part = dot(inputs, up_ref[...])
    grad_hidden = dot(scaled, down_ref[...])
    sigmoid_gate = jax.nn.sigmoid(gate_part)
    silu_gate = gate_part * sigmoid_gate
    hidden = silu_gate * up_part
    hidden_ref[...] = hidden.astype(BF16)
    pre_gate_ref[...] = (
        grad_hidden * up_part * sigmoid_gate * (1.0 + gate_part * (1.0 - sigmoid_gate))
    ).astype(BF16)
    pre_up_ref[...] = (grad_hidden * silu_gate).astype(BF16)
    total = jnp.broadcast_to(
        jnp.sum(hidden * grad_hidden, axis=1, keepdims=True), gate_sum_ref.shape
    )

    @pl.when(pl.program_id(0) == 0)
    def _():
        gate_sum_ref[...] = total

    @pl.when(pl.program_id(0) > 0)
    def _():
        gate_sum_ref[...] += total


def row_grads_kernel(place_ref, pre_gate_ref, pre_up_ref, gate_ref, up_ref, gate_sum_ref, back_ref):
    step = gate_ref.shape[0]
    at = pl.multiple_of(pl.program_id(0) * step, step)
    back_ref[:, pl.ds(at, step)] = (
        dot(pre_gate_ref[...], gate_ref[...], 1, 1) + dot(pre_up_ref[...], up_ref[...], 1, 1)
    ).astype(BF16)

    @pl.when(pl.program_id(0) == 0)
    def _():
        back_ref[:, back_ref.shape[1] - LANES :] = gate_sum_ref[...].astype(BF16)


def add(*terms):
    return sum([term.astype(F32) for term in terms])


def terms_kernel(place_ref, hidden_ref, pre_gate_ref, pre_up_ref, *refs, groups):
    operands = iter(refs[: len(refs) - len(groups)])
    hid = hidden_ref.shape[1]

    def first(inputs, scaled, own):
        return (dot(inputs, pre_gate_ref[...], 0, 0), dot(inputs, pre_up_ref[:, :own], 0, 0))

    def last(inputs, scaled, own):
        return (dot(inputs, pre_up_ref[:, own:], 0, 0), dot(scaled, hidden_ref[...], 0, 0))

    for (items, kind), out_ref in zip(groups, refs[len(refs) - len(groups) :]):
        part = out_ref.shape[-1]
        own = part - hid
        loaded = [
            (next(operands)[...], None if of_first else next(operands)[...])
            + tuple(next(operands) for _ in range(added))
            for _, _, of_first, added in items
        ]
        paired = len(items) == 2 and items[0][2] == items[1][2]
        if paired:
            inputs = jnp.concatenate([loaded[0][0], loaded[1][0]], axis=1)
            scaled = None if items[0][2] else jnp.concatenate([loaded[0][1], loaded[1][1]], axis=1)
            sums = (first if items[0][2] else last)(inputs, scaled, own)
            rows = inputs.shape[1] // 2
            results = [tuple(half[:rows] for half in sums), tuple(half[rows:] for half in sums)]
        else:
            results = [
                (first if item[2] else last)(load[0], load[1], own)
                for item, load in zip(items, loaded)
            ]
        for at, (item, load, result) in enumerate(zip(items, loaded, results)):
            start = 0
            for piece in result:
                end = start + piece.shape[1]
                for added in load[2:]:
                    piece = piece + added[0, :, start:end].astype(F32)
                out_ref[at, :, start:end] = piece.astype(kind)
                start = end


def joined_kernel(place_ref, kept_ref, other_ref, up_out, down_out):
    up_out[0] = add(kept_ref[0], other_ref[0]).astype(BF16)
    down_out[0] = add(kept_ref[1], other_ref[1]).astype(BF16)


def total_kernel(
    place_ref, base_ref, x_up_ref, x_down_ref, y_up_ref, y_down_ref, gate_up_ref, down_ref
):
    part = x_up_ref.shape[-1]
    wide = gate_up_ref.shape[-1]
    last = add(base_ref[1], x_down_ref[0], y_up_ref[0])
    gate_up_ref[0, :, :part] = add(base_ref[0], x_up_ref[0], y_down_ref[0])
    gate_up_ref[0, :, part:] = last[:, : wide - part]
    down_ref[0] = last[:, wide - part :]


def home_kernel(target_ref, gates_ref, back_ref, grads_ref, gate_grads_ref):
    slots, count = back_ref.shape[0], target_ref.shape[1]
    width = grads_ref.shape[1]
    slot = lax.broadcasted_iota(jnp.int32, (slots, count), 0)
    from_first = jnp.where(slot == target_ref[0:1, :], 1.0, 0.0).astype(BF16)
    from_second = jnp.where(slot == target_ref[1:2, :], 1.0, 0.0).astype(BF16)
    both = from_first + from_second
    step = 512
    for at in range(0, width, step):
        grads_ref[:, at : at + step] = dot(both, back_ref[:, at : at + step], 0, 0).astype(BF16)
    sums = back_ref[:, width : width + 128]
    first = dot(sums, from_first, 0, 0)[0:1, :]
    second = dot(sums, from_second, 0, 0)[0:1, :]
    gates = gates_ref[...].astype(F32)
    gate_grads_ref[0:1, :] = (first / gates[0:1, :]).astype(BF16)
    gate_grads_ref[1:2, :] = (second / gates[1:2, :]).astype(BF16)


def whole(shape):
    return pl.BlockSpec(shape, lambda i: (0,) * len(shape))


def shards(tokens, grad_out, expert_ids, gates, gate_up_weight, down_weight):
    count, top = expert_ids.shape
    width = tokens.shape[1]
    experts = lax.axis_size("blk")
    capacity = 2 * count * top // experts
    slots = experts * capacity
    gate_up, down = gate_up_weight[0], down_weight[0]
    hid = down.shape[1]
    ids_t, gates_t = expert_ids.T, gates.T
    ring = lax.axis_size("rep") // 2
    params = functools.partial(pltpu.CompilerParams, vmem_limit_bytes=48 * MIB)

    send, target, place = pl.pallas_call(
        functools.partial(dispatch_kernel, experts=experts, ring=ring),
        out_shape=(
            jax.ShapeDtypeStruct((slots, 2 * width), BF16),
            jax.ShapeDtypeStruct((top, count), jnp.int32),
            jax.ShapeDtypeStruct((2,), jnp.int32),
        ),
        out_specs=(
            pl.BlockSpec(memory_space=pltpu.VMEM),
            pl.BlockSpec(memory_space=pltpu.VMEM),
            pl.BlockSpec(memory_space=pltpu.SMEM),
        ),
        compiler_params=params(vmem_limit_bytes=60 * MIB),
        name="dispatch",
    )(ids_t, gates_t, tokens, grad_out)

    rows = lax.all_to_all(
        send.reshape(experts, capacity, 2 * width), "blk", split_axis=0, concat_axis=0, tiled=True
    ).reshape(slots, 2 * width)

    tile = 256
    steps = hid // tile
    hidden, pre_gate, pre_up, gate_sum = pl.pallas_call(
        rows_kernel,
        grid=(steps,),
        in_specs=[
            whole((slots, 2 * width)),
            pl.BlockSpec((width, tile), lambda i: (0, i)),
            pl.BlockSpec((width, tile), lambda i: (0, steps + i)),
            pl.BlockSpec((width, tile), lambda i: (0, i)),
        ],
        out_specs=[pl.BlockSpec((slots, tile), lambda i: (0, i))] * 3 + [whole((slots, LANES))],
        out_shape=[jax.ShapeDtypeStruct((slots, hid), BF16)] * 3
        + [jax.ShapeDtypeStruct((slots, LANES), F32)],
        compiler_params=params(),
        name="rows",
    )(rows, gate_up, gate_up, down)

    block = width // lax.axis_size("rep")

    def around(place, ahead):
        return lax.rem(place[0] + ahead, ring)

    def whole_p(shape):
        return pl.BlockSpec(shape, lambda i, p: (0,) * len(shape))

    anywhere = pl.BlockSpec(memory_space=pl.ANY)

    def call(kernel, name, grid, in_specs, out_specs, out_shape, *operands, after=(), cost=1):
        first = 1 + len(in_specs)

        def body(*refs):
            kernel(*refs[:first], *refs[first + len(after) : -1])
            refs[-1][...] = jnp.zeros_like(refs[-1])

        *outs, token = pl.pallas_call(
            body,
            grid_spec=pltpu.PrefetchScalarGridSpec(
                num_scalar_prefetch=1,
                grid=(grid,),
                in_specs=[*in_specs, *[anywhere] * len(after)],
                out_specs=[*out_specs, whole_p((8, 128))],
            ),
            out_shape=[*out_shape, jax.ShapeDtypeStruct((8, 128), F32)],
            compiler_params=params(),
            cost_estimate=pl.CostEstimate(flops=cost, bytes_accessed=1, transcendentals=0),
            name=name,
        )(place, *operands, *after)
        return outs, token

    def shape(*dims):
        return pltpu.HBM(dims, BF16)

    def permute(array, ahead):
        pairs = [
            (high * ring + low, high * ring + (low + ahead) % ring)
            for high in range(2)
            for low in range(ring)
        ]
        return lax.ppermute(array, "rep", pairs)

    def swap(array):
        pairs = [(at, (at + ring) % (2 * ring)) for at in range(2 * ring)]
        return lax.ppermute(array, "rep", pairs)

    far = ring // 2
    part = 3 * hid // 2

    def onward(pair):
        return permute(pair[0], 1), permute(pair[1], -1)

    def some_terms(name, groups, after=()):
        specs, operands, counted, outs, kinds = [], [], [], [], []
        for items, kind in groups:
            for half, ahead, of_first, added in items:
                for start in (0,) if of_first else (0, 2):

                    def at(i, p, half=half, ahead=ahead, start=start):
                        return 0, (start + half(p)) * ring + around(p, (ahead + ring) % ring)

                    specs.append(pl.BlockSpec((slots, block), at))
                    operands.append(rows)
                for array, place_of in added:

                    def at(i, p, place_of=place_of):
                        return place_of(p), 0, 0

                    specs.append(pl.BlockSpec((1, block, part), at))
                    operands.append(array)
            counted.append(([item[:3] + (len(item[3]),) for item in items], kind))
            outs.append(whole_p((len(items), block, part)))
            kinds.append(
                shape(len(items), block, part)
                if kind == BF16
                else jax.ShapeDtypeStruct((len(items), block, part), kind)
            )
        return call(
            functools.partial(terms_kernel, groups=counted),
            name,
            1,
            [whole_p((slots, hid))] * 3 + specs,
            outs,
            kinds,
            hidden, pre_gate, pre_up, *operands, after=after,
        )

    def low(p):
        return 0

    def high(p):
        return 1

    def mine(p):
        return p[1]

    def theirs(p):
        return 1 - p[1]

    def hop(name, at, up_first, pair, after):
        def both(ahead, of_first, array):
            return [
                (half, ahead, of_first, [] if array is None else [(array, half)])
                for half in (low, high)
            ], BF16

        up, down = pair or (None, None)
        return some_terms(
            name, [both(at, up_first, up), both(-at, not up_first, down)], after
        )

    def split_hop(name, at, up_first, pair, after):
        def one_half(half, kind):
            return [
                (half, at, up_first, [(pair[0], half)]),
                (half, -at, not up_first, [(pair[1], half)]),
            ], kind

        return some_terms(name, [one_half(mine, F32), one_half(theirs, BF16)], after)

    one = whole_p((1, block, part))
    pair_of = whole_p((2, block, part))

    def joined(name, kept, other, after, cost=1):
        return call(
            joined_kernel,
            name,
            1,
            [pair_of, pair_of],
            [one] * 2,
            [shape(1, block, part)] * 2,
            kept, other, after=after, cost=cost,
        )

    tile = 4 * block
    steps = width // tile
    sent, token = hop("first_x", far, True, None, ())
    x_pair = onward(sent)
    (sent,), token = some_terms(
        "own_theirs", [([(theirs, 0, True, []), (theirs, 0, False, [])], BF16)],
        (token,),
    )
    own_other = swap(sent)
    sent, token = hop("first_y", far - 1, False, None, (token,))
    y_pair = onward(sent)
    (back,), token = call(
        row_grads_kernel,
        "row_grads",
        steps,
        [
            whole_p((slots, hid)),
            whole_p((slots, hid)),
            pl.BlockSpec((tile, hid), lambda i, p: (i, 0)),
            pl.BlockSpec((tile, hid), lambda i, p: (i, 1)),
            whole_p((slots, LANES)),
        ],
        [whole_p((slots, width + LANES))],
        [shape(slots, width + LANES)],
        pre_gate, pre_up, gate_up, gate_up, gate_sum, after=(token,),
    )
    sent, token = hop("hop_x3", far - 1, True, x_pair, (token,))
    x_pair = onward(sent)
    sent, token = hop("hop_y2", far - 2, False, y_pair, (token,))
    y_pair = onward(sent)
    sent, token = hop("hop_x2", far - 2, True, x_pair, (token, own_other))
    x_pair = onward(sent)
    (y_kept, sent), token = split_hop("hop_y1", far - 3, False, y_pair, (token,))
    y_other = swap(sent)
    (base,), token = some_terms(
        "own",
        [
            (
                [
                    (mine, 0, True, [(own_other, low)]),
                    (mine, 0, False, [(own_other, high)]),
                ],
                F32,
            )
        ],
        (token,),
    )
    (x_kept, sent), token = split_hop("hop_x1", far - 3, True, x_pair, (token,))
    x_other = swap(sent)
    sent, token = joined("joined_y", y_kept, y_other, (token,))
    y_pair = onward(sent)
    sent, token = joined("joined_x", x_kept, x_other, (token,), TOTAL_COST)
    x_pair = onward(sent)
    (gate_up_total, down_total), _ = call(
        total_kernel,
        "total",
        1,
        [pair_of, one, one, one, one],
        [whole_p((1, block, 2 * hid)), whole_p((1, block, hid))],
        [
            jax.ShapeDtypeStruct((1, block, 2 * hid), F32),
            jax.ShapeDtypeStruct((1, block, hid), F32),
        ],
        base, *x_pair, *y_pair,
    )

    returned = lax.all_to_all(
        back.reshape(experts, capacity, width + LANES), "blk", split_axis=0, concat_axis=0, tiled=True
    ).reshape(slots, width + LANES)

    grad_tokens, gate_grads = pl.pallas_call(
        home_kernel,
        out_shape=(
            jax.ShapeDtypeStruct((count, width), BF16),
            jax.ShapeDtypeStruct((top, count), BF16),
        ),
        compiler_params=params(),
        name="home",
    )(target, gates_t, returned)
    return grad_tokens, gate_grads.T, gate_up_total, down_total


def solution(mesh):
    in_specs = (
        P(("blk", "rep"), None),
        P(("blk", "rep"), None),
        P(("blk", "rep"), None),
        P(("blk", "rep"), None),
        P("blk", None, None),
        P("blk", None, None),
    )
    out_specs = (
        P(("blk", "rep"), None),
        P(("blk", "rep"), None),
        P("blk", "rep", None),
        P("blk", "rep", None),
    )
    return jax.shard_map(shards, mesh=mesh, in_specs=in_specs, out_specs=out_specs, check_vma=False)
```
